32 devices in a mesh: parts: 2 (over x), expert: 16 (over z, y, core).
Axes of the slice: x: 2, y: 2, z: 4, core: 2. Of those that a mesh axis runs over, the one named last changes fastest.
Arguments:
- queries: bfloat16 [3072, 2048], P(('parts', 'expert')), parts along dimension 0, may hold values from -150 to 150
- kv_cache: bfloat16 [6144, 16, 512], P(('parts', 'expert')), parts along dimension 0, may hold values from -6 to 6
- new_kv: bfloat16 [3072, 512], P(('parts', 'expert')), parts along dimension 0, may hold values from -6 to 6
- page_table: int32 [3072, 16], P(('parts', 'expert')), parts along dimension 0, may hold values from 0 to 191, as said below
- ctx_len: int32 [3072], P(('parts', 'expert')), parts along dimension 0, may hold values from 2 to 256, as said below
- resid: bfloat16 [3072, 1024], P(('parts', 'expert')), parts along dimension 0, may hold values from -6 to 6
- w_out: bfloat16 [2048, 1024], replicated, may hold values from -0.125 to 0.125
- moe_gain: float32 [1024], replicated, may hold values from 0.25 to 1.75
- w_gate: bfloat16 [16, 1024, 768], P('expert'), may hold values from -0.1875 to 0.1875
- w_up: bfloat16 [16, 1024, 768], P('expert'), may hold values from -0.1875 to 0.1875
- w_down: bfloat16 [16, 768, 1024], P('expert'), may hold values from -0.21875 to 0.21875
- routes: int32 [3072, 8], P(('parts', 'expert')), parts along dimension 0, may hold values from 0 to 15, all different within a row; in each aligned block of 48 rows (0 to 47, 48 to 95, ...) at most 48 rows name the same one
- route_weight: float32 [3072, 8], P(('parts', 'expert')), parts along dimension 0, may hold values from 0.05 to 0.3
- talker_owner: int32 [3072], P(('parts', 'expert')), parts along dimension 0, may hold values from 0 to 15, as said below
- speaking: int32 [3072], P(('parts', 'expert')), parts along dimension 0, may hold values from 0 to 1
- codec_state: bfloat16 [3072, 1024], P(('parts', 'expert')), parts along dimension 0, may hold values from -6 to 6
- talk_gain: float32 [1024], replicated, may hold values from 0.25 to 1.75
- w_talk: bfloat16 [1024, 1024], replicated, may hold values from -0.1875 to 0.1875
Outputs:
- thinker_out: bfloat16 [3072, 1024], P(('parts', 'expert')), parts along dimension 0
- talker_out: bfloat16 [3072, 1024], P(('parts', 'expert')), parts along dimension 0
The draws below stay inside these ranges and needn't reach their ends.
There are 2 independent parts, one for each index of `parts`. The reference program is written for one: setup_inputs(seed, part) draws one part's arguments, and reference() takes and returns one part's arrays. A program takes and returns all parts, laid end to end along the dimension named above; an argument that names none is the same for every part. Nothing has to cross between parts.
Inputs may be any that keep to these rules, and one draw needn't show every extreme that they name: `page_table`: entries j < ceil(ctx_len[r] / 16) name pages of the pool of the device that holds request r, counted within that pool; live pages of different requests differ; other entries are 0. `ctx_len`: in every draw some request has 256 cached tokens. `routes`: each row names 8 different experts. In each aligned block of 48 rows no expert is named by more than 48 rows, and some block reaches that. `talker_owner`: among the speaking rows of one device at most 6 have the same owner; a device's rows are spread over the owners as evenly as possible, and some owner receives exactly 6 speaking rows from every device.
All inputs are finite; a program needn't handle non-finite values.
Results may differ from the reference program's by a relative error of at most 0.01.
Values may be sent and summed in bfloat16 or wider, within the bound.
A program may use at most 192 MiB of HBM per device.

```python
import math
import jax
import jax.numpy as jnp
import numpy as np
from jax import lax

D = 1024
QH = 16
KVH = 2
HD = 128
FF = 768
TOPK = 8
TW = 1024
PAGE = 16
MAXP = 16
REQ_DEV = 96
EXPERTS = 16
POOL_DEV = 192
HALF_CAP = 48
CAP = 96
TALK_CAP = 6
REQS = 1536
POOL = 3072
TSLOTS = 1536
N_EXPERT = 16


def pool_layout(key):
    base_key = jax.random.fold_in(key, 101)
    key_mult, key_span, key_device, key_request, key_order, key_fill = jax.random.split(base_key, 6)
    factor = 2 ** jax.random.randint(key_mult, (N_EXPERT,), 0, 3)
    reach_limit = jnp.maximum(1, MAXP * factor // 4)
    raw_extra = jax.random.randint(key_span, (N_EXPERT, REQ_DEV), 0, 1 << 20) % reach_limit[:, None]
    spare_pages = POOL_DEV - MAXP - REQ_DEV
    spread = jnp.sum(raw_extra, axis=1, keepdims=True)
    scaled = jnp.where(spread > spare_pages, raw_extra * spare_pages // jnp.maximum(spread, 1), raw_extra)
    page_count = 1 + scaled
    chosen_device = jax.random.randint(key_device, (), 0, N_EXPERT)
    chosen_request = jax.random.randint(key_request, (), 0, REQ_DEV)
    full_mask = (jnp.arange(N_EXPERT)[:, None] == chosen_device) & (jnp.arange(REQ_DEV)[None, :] == chosen_request)
    page_count = jnp.where(full_mask, MAXP, page_count)
    starts = jnp.cumsum(page_count, axis=1) - page_count
    orders = jax.vmap(lambda subkey: jax.random.permutation(subkey, POOL_DEV))(jax.random.split(key_order, N_EXPERT))
    slot_index = jnp.arange(MAXP)
    position = jnp.minimum(starts[:, :, None] + slot_index[None, None, :], POOL_DEV - 1)
    picked = jax.vmap(lambda ordering, where_at: ordering[where_at])(orders, position)
    table = jnp.where(slot_index[None, None, :] < page_count[:, :, None], picked, 0)
    last_fill = jax.random.randint(key_fill, (N_EXPERT, REQ_DEV), 2, PAGE + 1)
    lengths = jnp.where(full_mask, MAXP * PAGE, (page_count - 1) * PAGE + last_fill)
    return (table.reshape(REQS, MAXP).astype(jnp.int32), lengths.reshape(REQS).astype(jnp.int32))


def cache_values(key):
    return jax.random.truncated_normal(jax.random.fold_in(key, 202), -6.0, 6.0, (POOL, PAGE, 2 * KVH * HD), jnp.float32)


def draw_page_table(key, part):
    return pool_layout(key)[0]


def draw_ctx_len(key, part):
    return pool_layout(key)[1]


def draw_kv_cache(key, part):
    values = cache_values(key)
    return values.astype(jnp.bfloat16)


def draw_queries(key, part):
    values = jax.random.truncated_normal(jax.random.fold_in(key, 303), -6.0, 6.0, (REQS, QH * HD), jnp.float32)
    return values.astype(jnp.bfloat16)


def talker_layout(key):
    base_key = jax.random.fold_in(key, 404)
    key_base, key_rank, key_voice = jax.random.split(base_key, 3)
    anchor = jax.random.randint(key_base, (), 0, N_EXPERT)
    rank_table = jax.vmap(lambda subkey: jax.random.permutation(subkey, REQ_DEV))(jax.random.split(key_rank, N_EXPERT))
    owners = (anchor + rank_table) % N_EXPERT
    voiced = jnp.where(rank_table % N_EXPERT == 0, 1, (jax.random.randint(key_voice, (N_EXPERT, REQ_DEV), 0, 4) > 0).astype(jnp.int32))
    return (owners.reshape(REQS).astype(jnp.int32), voiced.reshape(REQS).astype(jnp.int32))


def draw_talker_owner(key, part):
    return talker_layout(key)[0]


def draw_speaking(key, part):
    return talker_layout(key)[1]


def levels(own_key, shape, shards, least, largest):
    factor_of, own = 1.0, jax.random.fold_in(own_key, 6)
    for dim, parts in shards:
        draws = jnp.exp(jax.random.uniform(jax.random.fold_in(own, dim), (parts,), jnp.float32, least / len(shards), largest / len(shards)))
        factor_of = factor_of * jnp.repeat(draws, shape[dim] // parts).reshape([-1 if axis == dim else 1 for axis in range(len(shape))])
    return factor_of


def shared_out(rng, own, number, rows, count, top, reach, slope):
    ranking = jax.random.permutation(rng, count)
    heavy_load, ordinary = portions_of(count, rows * top, reach, slope, True), portions_of(count, rows * top, reach, slope, False)
    places = jnp.arange(count)

    def named(sizes, turn):
        used = int((sizes > 0).sum())
        fixed = max(1, used // 4)
        moved = fixed + (places - fixed + turn * (used - fixed)) % max(1, count - fixed)
        return jnp.zeros((count,), jnp.int32).at[ranking[jnp.where(places < fixed, places, moved)]].set(jnp.asarray(sizes, jnp.int32))

    sizes = jnp.where(number % 4 == 0, named(heavy_load, number // 4), named(ordinary, number - number // 4 - 1))
    mixed = jax.random.permutation(jax.random.fold_in(own, 3), count)
    giver, taker = mixed[0:count // 2 * 2:2], mixed[1:count // 2 * 2:2]
    room = jnp.minimum(sizes[giver] - 1, reach - sizes[taker]) // 2
    room = jnp.where((giver == ranking[0]) | (taker == ranking[0]) | (sizes[taker] == 0), 0, jnp.maximum(room, 0))
    moved = jax.random.randint(jax.random.fold_in(own, 4), (count // 2,), 0, 1 << 20) % (room + 1)
    sizes = sizes.at[giver].add(-moved).at[taker].add(moved)
    members = jnp.searchsorted(jnp.cumsum(sizes), jnp.arange(rows * top), side="right").astype(jnp.int32)
    listing = members.reshape(top, rows).T
    listing = listing[jax.random.permutation(jax.random.fold_in(own, 1), rows)]
    turn = jax.random.randint(jax.random.fold_in(own, 2), (rows, 1), 0, top)
    return jnp.take_along_axis(listing, (jnp.arange(top)[None, :] + turn) % top, axis=1)


def portions_of(amount, total, reach, skew, full):
    portions = [(1 << 20) // math.isqrt(rank ** skew) + 1 for rank in range(1, amount + 1)]
    largest = reach if full else min(reach, max(-(-total // amount), total * portions[0] // sum(portions)))
    least = 1 if total - largest >= amount - 1 else 0
    holding, spare = [largest] + [least] * (amount - 1), total - largest - least * (amount - 1)
    while spare > 0:
        free = [i for i in range(1, amount) if holding[i] < largest] or [i for i in range(1, amount) if holding[i] < reach]
        whole, budget = sum([portions[i] for i in free]), spare
        for i in free:
            extra = min(reach - holding[i], max(1, budget * portions[i] // whole), spare)
            holding[i] = holding[i] + extra
            spare = spare - extra
    return np.array(holding)


def centred(stream_key, dims, scale, reach, cuts=(), kind=jnp.bfloat16):
    level = levels(stream_key, dims, cuts, -0.22, 0.18) if cuts else 1.0
    drawn = jax.random.normal(stream_key, dims, jnp.float32) * scale * level
    return jnp.minimum(jnp.maximum(drawn, -reach), reach).astype(kind)


def setup_inputs(seed: int = 0, part: int = 0) -> dict:
    keys = jax.random.split(jax.random.key(seed), 19)
    part_splits = jax.random.split(jax.random.fold_in(keys[18], part), 19)
    queries = draw_queries(jax.random.fold_in(jax.random.fold_in(keys[18], part), 71), part)
    kv_cache = draw_kv_cache(jax.random.fold_in(jax.random.fold_in(keys[18], part), 71), part)
    new_kv = centred(part_splits[2], (REQS, 2 * KVH * HD), 1.0, 6.0, ((0, 16),))
    page_table = draw_page_table(jax.random.fold_in(jax.random.fold_in(keys[18], part), 71), part)
    ctx_len = draw_ctx_len(jax.random.fold_in(jax.random.fold_in(keys[18], part), 71), part)
    resid = centred(part_splits[5], (REQS, D), 1.0, 6.0, ((0, 16),))
    w_out = centred(keys[6], (QH * HD, D), (QH * HD) ** -0.5, 0.125)
    moe_gain = jnp.clip(1.0 + 0.15 * jax.random.normal(keys[7], (D,), jnp.float32), 0.25, 1.75)
    w_gate = centred(keys[8], (EXPERTS, D, FF), D ** -0.5, 0.1875, ((0, 16),))
    w_up = centred(keys[9], (EXPERTS, D, FF), D ** -0.5, 0.1875, ((0, 16),))
    w_down = centred(keys[10], (EXPERTS, FF, D), FF ** -0.5, 0.21875, ((0, 16),))
    routes_keys = jax.random.split(jax.random.fold_in(part_splits[11], 1), REQS // (REQ_DEV // 2))
    routes_turns = jax.random.permutation(jax.random.fold_in(part_splits[11], 3), REQS // (REQ_DEV // 2))
    routes = jax.vmap(lambda own, number: shared_out(jax.random.fold_in(part_splits[11], 2), own, number, REQ_DEV // 2, EXPERTS, TOPK, HALF_CAP, 2))(routes_keys, routes_turns).reshape((REQS, TOPK))
    route_weight = jnp.clip(0.05 + 0.25 * jax.random.uniform(part_splits[12], (REQS, TOPK), jnp.float32) ** levels(part_splits[12], (REQS, TOPK), ((0, 16),), -0.2, 0.2), 0.05, 0.3)
    talker_owner = draw_talker_owner(jax.random.fold_in(jax.random.fold_in(keys[18], part), 71), part)
    speaking = draw_speaking(jax.random.fold_in(jax.random.fold_in(keys[18], part), 71), part)
    codec_state = centred(part_splits[15], (TSLOTS, TW), 1.0, 6.0, ((0, 16),))
    talk_gain = jnp.clip(1.0 + 0.15 * jax.random.normal(keys[16], (D,), jnp.float32), 0.25, 1.75)
    w_talk = centred(keys[17], (D, TW), D ** -0.5, 0.1875)
    return {"queries": queries, "kv_cache": kv_cache, "new_kv": new_kv, "page_table": page_table, "ctx_len": ctx_len, "resid": resid, "w_out": w_out, "moe_gain": moe_gain, "w_gate": w_gate, "w_up": w_up, "w_down": w_down, "routes": routes, "route_weight": route_weight, "talker_owner": talker_owner, "speaking": speaking, "codec_state": codec_state, "talk_gain": talk_gain, "w_talk": w_talk}


def rms_scaled(values, gain_row):
    widened = values.astype(jnp.float32)
    return widened * lax.rsqrt(lax.optimization_barrier(jnp.mean(widened * widened, axis=-1, keepdims=True)) + 1e-06) * gain_row.astype(jnp.float32)

def attend(queries, pages, lengths, fresh):
    row_total = queries.shape[0]
    context_span = MAXP * PAGE
    groups = QH // KVH
    stacked = pages.reshape(row_total, context_span, 2 * KVH * HD).astype(jnp.float32)
    cached_keys = stacked[:, :, :KVH * HD].reshape(row_total, context_span, KVH, HD)
    cached_values = stacked[:, :, KVH * HD:].reshape(row_total, context_span, KVH, HD)
    query_heads = queries.astype(jnp.float32).reshape(row_total, KVH, groups, HD)
    scaling = 1.0 / math.sqrt(HD)
    scores = jnp.einsum('rkgd,rlkd->rkgl', query_heads, cached_keys) * scaling
    live_mask = jnp.arange(context_span, dtype=jnp.int32)[None, :] < lengths[:, None]
    scores = jnp.where(live_mask[:, None, None, :], scores, -jnp.inf)
    fresh_wide = fresh.astype(jnp.float32)
    fresh_keys = fresh_wide[:, :KVH * HD].reshape(row_total, KVH, HD)
    fresh_values = fresh_wide[:, KVH * HD:].reshape(row_total, KVH, HD)
    own_score = jnp.einsum('rkgd,rkd->rkg', query_heads, fresh_keys) * scaling
    highest = jnp.maximum(lax.optimization_barrier(jnp.max(scores, axis=-1)), own_score)
    weights = jnp.exp(scores - highest[..., None])
    own_weight = jnp.exp(own_score - highest)
    denominator = lax.optimization_barrier(jnp.sum(weights, axis=-1)) + own_weight
    probabilities = (weights / denominator[..., None]).astype(jnp.bfloat16)
    own_prob = (own_weight / denominator).astype(jnp.bfloat16)
    mixture = jnp.einsum('rkgl,rlkd->rkgd', probabilities.astype(jnp.float32), cached_values)
    mixture = mixture + own_prob.astype(jnp.float32)[..., None] * fresh_values[:, :, None, :]
    return mixture.reshape(row_total, QH * HD).astype(jnp.bfloat16)

def reference(queries, kv_cache, new_kv, page_table, ctx_len, resid, w_out, moe_gain, w_gate, w_up, w_down, routes, route_weight, talker_owner, speaking, codec_state, talk_gain, w_talk):
    blocks = (kv_cache.reshape(N_EXPERT, POOL_DEV, PAGE, 2 * KVH * HD), queries.reshape(N_EXPERT, REQ_DEV, QH * HD), page_table.reshape(N_EXPERT, REQ_DEV, MAXP), ctx_len.reshape(N_EXPERT, REQ_DEV), new_kv.reshape(N_EXPERT, REQ_DEV, 2 * KVH * HD))

    def per_device(packed):
        pool_block, query_block, table_block, length_block, fresh_block = packed
        return attend(query_block, pool_block[table_block], length_block, fresh_block)
    attended = lax.map(per_device, blocks).reshape(REQS, QH * HD)
    hidden = (resid.astype(jnp.float32) + jnp.dot(attended, w_out, preferred_element_type=jnp.float32)).astype(jnp.bfloat16)
    normed = rms_scaled(hidden, moe_gain).astype(jnp.bfloat16)
    pair_count = REQS * TOPK
    flat_routes = routes.reshape(-1)
    padded = jnp.concatenate([normed, jnp.zeros((1, D), jnp.bfloat16)], axis=0)
    most_rows = N_EXPERT * CAP

    def expert_step(results, expert):
        chosen = flat_routes == expert
        position = jnp.cumsum(chosen.astype(jnp.int32)) - 1
        target = jnp.where(chosen, position, most_rows)
        pair_ids = jnp.full((most_rows,), pair_count, jnp.int32).at[target].set(jnp.arange(pair_count, dtype=jnp.int32), mode='drop')
        inputs = padded[pair_ids // TOPK]
        gate_values = jnp.dot(inputs, w_gate[expert], preferred_element_type=jnp.float32)
        up_values = jnp.dot(inputs, w_up[expert], preferred_element_type=jnp.float32)
        activated = (jax.nn.silu(gate_values) * up_values).astype(jnp.bfloat16)
        output = jnp.dot(activated, w_down[expert], preferred_element_type=jnp.float32).astype(jnp.bfloat16)
        return (results.at[pair_ids].set(output, mode='drop'), None)
    results, unused = lax.scan(expert_step, jnp.zeros((pair_count, D), jnp.bfloat16), jnp.arange(EXPERTS, dtype=jnp.int32))
    mixture = lax.optimization_barrier(jnp.sum(route_weight[..., None] * results.reshape(REQS, TOPK, D).astype(jnp.float32), axis=1))
    thinker_out = (hidden.astype(jnp.float32) + mixture).astype(jnp.bfloat16)
    voice_in = rms_scaled(thinker_out, talk_gain).astype(jnp.bfloat16)
    projected = jnp.dot(voice_in, w_talk, preferred_element_type=jnp.float32)
    owner_block = talker_owner.reshape(N_EXPERT, REQ_DEV)
    voiced_block = speaking.reshape(N_EXPERT, REQ_DEV)
    one_hot = ((owner_block[:, :, None] == jnp.arange(N_EXPERT, dtype=jnp.int32)[None, None, :]) & (voiced_block[:, :, None] == 1)).astype(jnp.int32)
    earlier = lax.optimization_barrier(jnp.sum((jnp.cumsum(one_hot, axis=1) - one_hot) * one_hot, axis=2))
    slot_ids = owner_block * (N_EXPERT * TALK_CAP) + jnp.arange(N_EXPERT, dtype=jnp.int32)[:, None] * TALK_CAP + earlier
    slot_ids = jnp.where(voiced_block == 1, slot_ids, TSLOTS).reshape(REQS).astype(jnp.int32)
    talker_out = codec_state.astype(jnp.float32).at[slot_ids].add(projected, mode='drop').astype(jnp.bfloat16)
    return (thinker_out, talker_out)
```

```python
import functools
import math

import jax
import jax.numpy as jnp
from jax import lax
from jax.experimental import pallas as pl
from jax.experimental.pallas import tpu as pltpu
from jax.sharding import PartitionSpec as P

HD = 128
STACK = 4
NEG = -1e30
LOG2E = 1.4426950408889634


def attend_kernel(
    kv_heads,
    page,
    q_ref,
    kv_ref,
    fresh_ref,
    table_ref,
    len_ref,
    resid_ref,
    wout_ref,
    gain_ref,
    hidden_ref,
    normed_ref,
    bias_ref,
    att_ref,
):
    rows, qwidth = q_ref.shape
    tokens = kv_ref.shape[0]
    pages = tokens // page
    max_pages = table_ref.shape[1]
    heads = qwidth // HD
    per_kv = heads // kv_heads
    factor = LOG2E / math.sqrt(HD)

    lengths = len_ref[...]
    page_ids = lax.broadcasted_iota(jnp.int32, (rows, pages), 1)
    whole = jnp.zeros((rows, pages), jnp.float32)
    last = jnp.zeros((rows, pages), jnp.float32)
    for j in range(max_pages):
        named = page_ids == table_ref[:, j : j + 1]
        whole += jnp.where(named & (lengths >= page * (j + 1)), 1.0, 0.0)
        last += jnp.where(
            named & (lengths > page * j) & (lengths < page * (j + 1)), 1.0, 0.0
        )
    spread = jnp.where(
        lax.broadcasted_iota(jnp.int32, (pages, tokens), 1) // page
        == lax.broadcasted_iota(jnp.int32, (pages, tokens), 0),
        1.0,
        0.0,
    ).astype(jnp.bfloat16)
    whole_tok = jnp.dot(whole.astype(jnp.bfloat16), spread, preferred_element_type=jnp.float32)
    last_tok = jnp.dot(last.astype(jnp.bfloat16), spread, preferred_element_type=jnp.float32)
    place = lax.rem(lax.broadcasted_iota(jnp.int32, (rows, tokens), 1), page)
    times = whole_tok + jnp.where(place < lax.rem(lengths, page), last_tok, 0.0)
    bias_ref[...] = jnp.where(times > 0.5, jnp.log2(jnp.maximum(times, 1.0)), NEG)

    def step(i, carry):
        kvh = (i * STACK) // per_kv
        lanes = pl.ds(pl.multiple_of(i * STACK * HD, STACK * HD), STACK * HD)
        keys = pl.ds(pl.multiple_of(kvh * HD, HD), HD)
        vals = pl.ds(pl.multiple_of((kv_heads + kvh) * HD, HD), HD)
        qs = q_ref[:, lanes]
        stacked = jnp.concatenate([qs[:, h * HD : (h + 1) * HD] for h in range(STACK)], axis=0)
        scores = lax.dot_general(
            stacked, kv_ref[:, keys], (((1,), (1,)), ((), ())), preferred_element_type=jnp.float32
        )
        fresh_key = fresh_ref[:, keys].astype(jnp.float32)
        fresh_val = fresh_ref[:, vals].astype(jnp.float32)
        wide = stacked.astype(jnp.float32).reshape(STACK, rows, HD)
        own = jnp.sum(wide * fresh_key[None], axis=-1, keepdims=True) * factor
        logits = scores.reshape(STACK, rows, tokens) * factor + bias_ref[...][None]
        highest = jnp.maximum(jnp.max(logits, axis=-1, keepdims=True), own)
        weights = jnp.exp2(logits - highest)
        own_weight = jnp.exp2(own - highest)
        denom = jnp.sum(weights, axis=-1, keepdims=True) + own_weight
        mixed = jnp.dot(
            weights.astype(jnp.bfloat16).reshape(STACK * rows, tokens),
            kv_ref[:, vals],
            preferred_element_type=jnp.float32,
        ).reshape(STACK, rows, HD)
        mixed = ((mixed + own_weight * fresh_val[None]) / denom).astype(jnp.bfloat16)
        att_ref[:, lanes] = jnp.concatenate([mixed[h] for h in range(STACK)], axis=1)
        return carry

    lax.fori_loop(0, heads // STACK, step, 0)
    hidden = (
        resid_ref[...].astype(jnp.float32)
        + jnp.dot(att_ref[...], wout_ref[...], preferred_element_type=jnp.float32)
    ).astype(jnp.bfloat16)
    hidden_ref[...] = hidden
    normed_ref[...] = rms_scaled(hidden, gain_ref[...]).astype(jnp.bfloat16)


def rms_scaled(values, gain_row):
    widened = values.astype(jnp.float32)
    return (
        widened * lax.rsqrt(jnp.mean(widened * widened, axis=-1, keepdims=True) + 1e-06) * gain_row
    )


def attend(queries, kv_cache, new_kv, page_table, ctx_len, resid, w_out, moe_gain):
    rows, width = resid.shape
    pages, page, kv_width = kv_cache.shape
    tokens = pages * page
    shape = jax.ShapeDtypeStruct((rows, width), jnp.bfloat16)
    return pl.pallas_call(
        functools.partial(attend_kernel, kv_width // (2 * HD), page),
        out_shape=(shape, shape),
        in_specs=[pl.BlockSpec(memory_space=pltpu.VMEM)] * 8,
        out_specs=(pl.BlockSpec(memory_space=pltpu.VMEM),) * 2,
        scratch_shapes=[
            pltpu.VMEM((rows, tokens), jnp.float32),
            pltpu.VMEM((rows, queries.shape[1]), jnp.bfloat16),
        ],
        compiler_params=pltpu.CompilerParams(vmem_limit_bytes=48 * 1024 * 1024),
        cost_estimate=pl.CostEstimate(
            flops=4 * rows * queries.shape[1] * tokens,
            bytes_accessed=2 * (tokens * kv_width + w_out.size + 4 * resid.size),
            transcendentals=0,
        ),
    )(
        queries,
        kv_cache.reshape(tokens, kv_width),
        new_kv,
        page_table,
        ctx_len[:, None],
        resid,
        w_out,
        moe_gain[None, :],
    )


def talker_pick(owners, voiced, devices, capacity):
    row_total = owners.shape[0]
    one_hot = (owners[:, None] == jnp.arange(devices, dtype=jnp.int32)[None, :]) & (
        voiced[:, None] == 1
    )
    order = jnp.arange(row_total, dtype=jnp.int32)
    before = (order[None, :] < order[:, None]).astype(jnp.bfloat16)
    counts = jnp.dot(before, one_hot.astype(jnp.bfloat16), preferred_element_type=jnp.float32)
    earlier = jnp.sum(jnp.where(one_hot, counts, 0.0), axis=1).astype(jnp.int32)
    target = jnp.where(voiced == 1, owners * capacity + earlier, devices * capacity)
    slots = jnp.arange(devices * capacity, dtype=jnp.int32)
    return (slots[:, None] == target[None, :]).astype(jnp.bfloat16)


def body(
    queries,
    kv_cache,
    new_kv,
    page_table,
    ctx_len,
    resid,
    w_out,
    moe_gain,
    w_gate,
    w_up,
    w_down,
    routes,
    route_weight,
    talker_owner,
    speaking,
    codec_state,
    talk_gain,
    w_talk,
):
    devices = lax.axis_size("expert")
    capacity = codec_state.shape[0] // devices
    local = w_gate.shape[0]
    experts = local * devices
    width = resid.shape[1]
    dense = jnp.sum(
        jnp.where(
            routes[:, :, None] == jnp.arange(experts, dtype=jnp.int32)[None, None, :],
            route_weight[:, :, None],
            0.0,
        ),
        axis=1,
    )
    dense_all = lax.all_gather(dense, "expert", axis=0, tiled=True)
    hidden, normed = attend(
        queries, kv_cache, new_kv, page_table, ctx_len, resid, w_out, moe_gain
    )
    everyone = lax.all_gather(normed, "expert", axis=0, tiled=True)
    me = lax.axis_index("expert")
    partial = 0.0
    for e in range(local):
        mine = jnp.arange(experts, dtype=jnp.int32) == me * local + e
        scale = jnp.sum(jnp.where(mine[None, :], dense_all, 0.0), axis=1, keepdims=True)
        gate_values = jnp.dot(everyone, w_gate[e], preferred_element_type=jnp.float32)
        up_values = jnp.dot(everyone, w_up[e], preferred_element_type=jnp.float32)
        activated = (jax.nn.silu(gate_values) * up_values).astype(jnp.bfloat16)
        partial = partial + scale * jnp.dot(
            activated, w_down[e], preferred_element_type=jnp.float32
        )
    mixture = lax.psum_scatter(
        partial.astype(jnp.bfloat16), "expert", scatter_dimension=0, tiled=True
    )
    thinker_out = (hidden.astype(jnp.float32) + mixture.astype(jnp.float32)).astype(jnp.bfloat16)
    voice_in = rms_scaled(thinker_out, talk_gain).astype(jnp.bfloat16)
    pick = talker_pick(talker_owner, speaking, devices, capacity)
    outgoing_voice = (
        jnp.dot(pick, voice_in, preferred_element_type=jnp.float32)
        .astype(jnp.bfloat16)
        .reshape(devices, capacity, width)
    )
    arrived = lax.all_to_all(outgoing_voice, "expert", split_axis=0, concat_axis=0, tiled=True)
    projected = jnp.dot(
        arrived.reshape(devices * capacity, width), w_talk, preferred_element_type=jnp.float32
    )
    talker_out = (codec_state.astype(jnp.float32) + projected).astype(jnp.bfloat16)
    return (thinker_out, talker_out)


def solution(mesh):
    both = ("parts", "expert")
    in_specs = (
        P(both, None),
        P(both, None, None),
        P(both, None),
        P(both, None),
        P(both),
        P(both, None),
        P(),
        P(),
        P("expert", None, None),
        P("expert", None, None),
        P("expert", None, None),
        P(both, None),
        P(both, None),
        P(both),
        P(both),
        P(both, None),
        P(),
        P(),
    )
    out_specs = (P(both, None), P(both, None))
    return jax.shard_map(body, mesh=mesh, in_specs=in_specs, out_specs=out_specs, check_vma=False)
```

```python
import functools
import math

import jax
import jax.numpy as jnp
from jax import lax
from jax.experimental import pallas as pl
from jax.experimental.pallas import tpu as pltpu
from jax.sharding import PartitionSpec as P

HD = 128
STACK = 4
NEG = -1e30
LOG2E = 1.4426950408889634


def attend_kernel(
    kv_heads,
    page,
    q_ref,
    kv_ref,
    fresh_ref,
    table_ref,
    len_ref,
    resid_ref,
    wout_ref,
    gain_ref,
    hidden_ref,
    normed_ref,
    bias_ref,
    att_ref,
):
    rows, qwidth = q_ref.shape
    tokens = kv_ref.shape[0]
    pages = tokens // page
    max_pages = table_ref.shape[1]
    heads = qwidth // HD
    per_kv = heads // kv_heads
    factor = LOG2E / math.sqrt(HD)

    lengths = len_ref[...]
    page_ids = lax.broadcasted_iota(jnp.int32, (rows, pages), 1)
    whole = jnp.zeros((rows, pages), jnp.float32)
    last = jnp.zeros((rows, pages), jnp.float32)
    for j in range(max_pages):
        named = page_ids == table_ref[:, j : j + 1]
        whole += jnp.where(named & (lengths >= page * (j + 1)), 1.0, 0.0)
        last += jnp.where(
            named & (lengths > page * j) & (lengths < page * (j + 1)), 1.0, 0.0
        )
    spread = jnp.where(
        lax.broadcasted_iota(jnp.int32, (pages, tokens), 1) // page
        == lax.broadcasted_iota(jnp.int32, (pages, tokens), 0),
        1.0,
        0.0,
    ).astype(jnp.bfloat16)
    whole_tok = jnp.dot(whole.astype(jnp.bfloat16), spread, preferred_element_type=jnp.float32)
    last_tok = jnp.dot(last.astype(jnp.bfloat16), spread, preferred_element_type=jnp.float32)
    place = lax.rem(lax.broadcasted_iota(jnp.int32, (rows, tokens), 1), page)
    times = whole_tok + jnp.where(place < lax.rem(lengths, page), last_tok, 0.0)
    bias_ref[...] = jnp.where(times > 0.5, jnp.log2(jnp.maximum(times, 1.0)), NEG)

    def step(i, carry):
        kvh = (i * STACK) // per_kv
        lanes = pl.ds(pl.multiple_of(i * STACK * HD, STACK * HD), STACK * HD)
        keys = pl.ds(pl.multiple_of(kvh * HD, HD), HD)
        vals = pl.ds(pl.multiple_of((kv_heads + kvh) * HD, HD), HD)
        qs = q_ref[:, lanes]
        stacked = jnp.concatenate([qs[:, h * HD : (h + 1) * HD] for h in range(STACK)], axis=0)
        scores = lax.dot_general(
            stacked, kv_ref[:, keys], (((1,), (1,)), ((), ())), preferred_element_type=jnp.float32
        )
        fresh_key = fresh_ref[:, keys].astype(jnp.float32)
        fresh_val = fresh_ref[:, vals].astype(jnp.float32)
        wide = stacked.astype(jnp.float32).reshape(STACK, rows, HD)
        own = jnp.sum(wide * fresh_key[None], axis=-1, keepdims=True) * factor
        logits = scores.reshape(STACK, rows, tokens) * factor + bias_ref[...][None]
        highest = jnp.maximum(jnp.max(logits, axis=-1, keepdims=True), own)
        weights = jnp.exp2(logits - highest)
        own_weight = jnp.exp2(own - highest)
        denom = jnp.sum(weights, axis=-1, keepdims=True) + own_weight
        mixed = jnp.dot(
            weights.astype(jnp.bfloat16).reshape(STACK * rows, tokens),
            kv_ref[:, vals],
            preferred_element_type=jnp.float32,
        ).reshape(STACK, rows, HD)
        mixed = ((mixed + own_weight * fresh_val[None]) / denom).astype(jnp.bfloat16)
        att_ref[:, lanes] = jnp.concatenate([mixed[h] for h in range(STACK)], axis=1)
        return carry

    lax.fori_loop(0, heads // STACK, step, 0)
    hidden = (
        resid_ref[...].astype(jnp.float32)
        + jnp.dot(att_ref[...], wout_ref[...], preferred_element_type=jnp.float32)
    ).astype(jnp.bfloat16)
    hidden_ref[...] = hidden
    normed_ref[...] = rms_scaled(hidden, gain_ref[...]).astype(jnp.bfloat16)


def rms_scaled(values, gain_row):
    widened = values.astype(jnp.float32)
    return (
        widened * lax.rsqrt(jnp.mean(widened * widened, axis=-1, keepdims=True) + 1e-06) * gain_row
    )


def attend(queries, kv_cache, new_kv, page_table, ctx_len, resid, w_out, moe_gain):
    rows, width = resid.shape
    pages, page, kv_width = kv_cache.shape
    tokens = pages * page
    shape = jax.ShapeDtypeStruct((rows, width), jnp.bfloat16)
    return pl.pallas_call(
        functools.partial(attend_kernel, kv_width // (2 * HD), page),
        out_shape=(shape, shape),
        in_specs=[pl.BlockSpec(memory_space=pltpu.VMEM)] * 8,
        out_specs=(pl.BlockSpec(memory_space=pltpu.VMEM),) * 2,
        scratch_shapes=[
            pltpu.VMEM((rows, tokens), jnp.float32),
            pltpu.VMEM((rows, queries.shape[1]), jnp.bfloat16),
        ],
        compiler_params=pltpu.CompilerParams(vmem_limit_bytes=48 * 1024 * 1024),
        cost_estimate=pl.CostEstimate(
            flops=4 * rows * queries.shape[1] * tokens,
            bytes_accessed=2 * (tokens * kv_width + w_out.size + 4 * resid.size),
            transcendentals=0,
        ),
    )(
        queries,
        kv_cache.reshape(tokens, kv_width),
        new_kv,
        page_table,
        ctx_len[:, None],
        resid,
        w_out,
        moe_gain[None, :],
    )


def flipped(me, bits, total):
    out, stride = 0, 1
    while stride < total:
        bit = (me // stride) % 2
        out = out + stride * ((1 - bit) if bits & stride else bit)
        stride *= 2
    return out


def finish_kernel(
    n,
    capacity,
    part_ref,
    hidden_ref,
    picks_ref,
    gain_ref,
    codec_ref,
    wtalk_ref,
    thinker_ref,
    talker_ref,
    stage,
    landed,
    voice_out,
    voice_in,
    send_sem,
    recv_sem,
    voice_send,
    voice_recv,
):
    rows, width = hidden_ref.shape
    cols = width // 2
    room = voice_out.shape[1]
    me = lax.axis_index("expert")
    barrier = pltpu.get_barrier_semaphore()

    def greet(i, carry):
        peer = (me + i) % n
        pl.semaphore_signal(
            barrier, inc=1, device_id={"expert": peer}, device_id_type=pl.DeviceIdType.MESH
        )
        return carry

    lax.fori_loop(1, n, greet, 0)
    pl.semaphore_wait(barrier, n - 1)

    strides = [1 << b for b in range(n.bit_length() - 1)]
    orders = (strides, strides[:1] + strides[2:] + strides[1:2])

    def step_of(half, r):
        return next(k for k, s in enumerate(orders[half]) if r & s)

    def message(half, r, source):
        partner = flipped(me, orders[half][step_of(half, r)], n)
        return pltpu.make_async_remote_copy(
            src_ref=source,
            dst_ref=landed.at[half, r],
            send_sem=send_sem.at[half, r],
            recv_sem=recv_sem.at[half, r],
            device_id={"expert": partner},
            device_id_type=pl.DeviceIdType.MESH,
        )

    def summed(half, r, k):
        lanes = slice(half * cols, (half + 1) * cols)
        total = part_ref[flipped(me, r, n), :, lanes].astype(jnp.float32)
        for j in range(k):
            m = r + orders[half][j]
            sent[half, m].wait_recv()
            total = total + landed[half, m].astype(jnp.float32)
        return total

    sent = {}
    for k in range(len(strides)):
        for half in range(2):
            todo = [r for r in range(1, n) if step_of(half, r) == k]
            nearer = orders[half][k + 1 :]
            todo.sort(key=lambda r: [-((r & s) > 0) for s in nearer])
            for r in todo:
                if k == 0:
                    source = part_ref.at[flipped(me, r, n), :, pl.ds(half * cols, cols)]
                else:
                    stage[half, r] = summed(half, r, k).astype(jnp.bfloat16)
                    source = stage.at[half, r]
                sent[half, r] = message(half, r, source)
                sent[half, r].start()
    mixture = jnp.concatenate([summed(half, 0, len(strides)) for half in range(2)], axis=1)
    thinker = (hidden_ref[...].astype(jnp.float32) + mixture).astype(jnp.bfloat16)
    thinker_ref[...] = thinker
    voice = rms_scaled(thinker, gain_ref[...]).astype(jnp.bfloat16)
    packed = jnp.dot(picks_ref[0], voice[:, :cols], preferred_element_type=jnp.float32) + jnp.dot(
        picks_ref[1], voice[:, cols:], preferred_element_type=jnp.float32
    )
    voice_out[...] = packed.astype(jnp.bfloat16).reshape(n, room, cols)
    voice_in[pl.ds(me, 1)] = voice_out[pl.ds(me, 1)]

    def voice_copy(i):
        peer = (me + i) % n
        return pltpu.make_async_remote_copy(
            src_ref=voice_out.at[peer],
            dst_ref=voice_in.at[me],
            send_sem=voice_send.at[i],
            recv_sem=voice_recv.at[i],
            device_id={"expert": peer},
            device_id_type=pl.DeviceIdType.MESH,
        )

    def begin(i, carry):
        voice_copy(i).start()
        return carry

    def end(i, carry):
        copy = voice_copy(i)
        copy.wait_send()
        copy.wait_recv()
        return carry

    lax.fori_loop(1, n, begin, 0)
    for copy in sent.values():
        copy.wait_send()
    lax.fori_loop(1, n, end, 0)
    arrived = voice_in[...].reshape(n * room, cols)
    slot = lax.broadcasted_iota(jnp.int32, (n * capacity, n * room), 0)
    place = lax.broadcasted_iota(jnp.int32, (n * capacity, n * room), 1)
    near = (slot // capacity) * room + lax.rem(slot, capacity)
    total = codec_ref[...].astype(jnp.float32)
    for half in range(2):
        chosen = jnp.where(place == near + half * (room // 2), 1.0, 0.0).astype(jnp.bfloat16)
        part = jnp.dot(chosen, arrived, preferred_element_type=jnp.float32).astype(jnp.bfloat16)
        total = total + jnp.dot(
            part, wtalk_ref[half * cols : (half + 1) * cols, :], preferred_element_type=jnp.float32
        )
    talker_ref[...] = total.astype(jnp.bfloat16)


def finish(n, capacity, partial, hidden, picks, talk_gain, codec_state, w_talk):
    rows, width = hidden.shape
    room = picks.shape[1] // n
    cols = width // 2
    return pl.pallas_call(
        functools.partial(finish_kernel, n, capacity),
        out_shape=(
            jax.ShapeDtypeStruct((rows, width), jnp.bfloat16),
            jax.ShapeDtypeStruct(codec_state.shape, jnp.bfloat16),
        ),
        in_specs=[pl.BlockSpec(memory_space=pltpu.VMEM)] * 6,
        out_specs=(pl.BlockSpec(memory_space=pltpu.VMEM),) * 2,
        scratch_shapes=[
            pltpu.VMEM((2, n, rows, cols), jnp.bfloat16),
            pltpu.VMEM((2, n, rows, cols), jnp.bfloat16),
            pltpu.VMEM((n, room, cols), jnp.bfloat16),
            pltpu.VMEM((n, room, cols), jnp.bfloat16),
            pltpu.SemaphoreType.DMA((2, n)),
            pltpu.SemaphoreType.DMA((2, n)),
            pltpu.SemaphoreType.DMA((n,)),
            pltpu.SemaphoreType.DMA((n,)),
        ],
        compiler_params=pltpu.CompilerParams(
            collective_id=0, has_side_effects=True, vmem_limit_bytes=56 * 1024 * 1024
        ),
    )(partial.reshape(n, rows, width), hidden, picks, talk_gain[None, :], codec_state, w_talk)


def talker_picks(owners, voiced, devices, capacity):
    row_total = owners.shape[0]
    span = -(-capacity // 8) * 8
    one_hot = (owners[:, None] == jnp.arange(devices, dtype=jnp.int32)[None, :]) & (
        voiced[:, None] == 1
    )
    order = jnp.arange(row_total, dtype=jnp.int32)
    before = (order[None, :] < order[:, None]).astype(jnp.bfloat16)
    counts = jnp.dot(before, one_hot.astype(jnp.bfloat16), preferred_element_type=jnp.float32)
    earlier = jnp.sum(jnp.where(one_hot, counts, 0.0), axis=1).astype(jnp.int32)
    room = 2 * span
    target = jnp.where(voiced == 1, owners * room + earlier, -room)
    slots = jnp.arange(devices * room, dtype=jnp.int32)
    return jnp.stack(
        [
            (slots[:, None] == target[None, :] + half * span).astype(jnp.bfloat16)
            for half in range(2)
        ]
    )


def body(
    queries,
    kv_cache,
    new_kv,
    page_table,
    ctx_len,
    resid,
    w_out,
    moe_gain,
    w_gate,
    w_up,
    w_down,
    routes,
    route_weight,
    talker_owner,
    speaking,
    codec_state,
    talk_gain,
    w_talk,
):
    devices = lax.axis_size("expert")
    capacity = codec_state.shape[0] // devices
    local = w_gate.shape[0]
    experts = local * devices
    width = resid.shape[1]
    dense = jnp.sum(
        jnp.where(
            routes[:, :, None] == jnp.arange(experts, dtype=jnp.int32)[None, None, :],
            route_weight[:, :, None],
            0.0,
        ),
        axis=1,
    )
    coarse = lax.reduce_precision(dense, 8, 7)
    wide = -(-2 * experts // 128) * 128
    riders = jnp.concatenate([coarse, dense - coarse], axis=1).astype(jnp.bfloat16)
    riders = jnp.pad(riders, ((0, 0), (0, wide - 2 * experts)))
    picks = talker_picks(talker_owner, speaking, devices, capacity)
    hidden, normed = attend(
        queries, kv_cache, new_kv, page_table, ctx_len, resid, w_out, moe_gain
    )
    gathered = lax.all_gather(
        jnp.concatenate([normed, riders], axis=1), "expert", axis=0, tiled=True
    )
    everyone = gathered[:, :width]
    shares = gathered[:, width : width + 2 * experts].astype(jnp.float32)
    me = lax.axis_index("expert")
    partial = 0.0
    for e in range(local):
        mine = jnp.arange(2 * experts, dtype=jnp.int32) % experts == me * local + e
        scale = jnp.sum(jnp.where(mine[None, :], shares, 0.0), axis=1, keepdims=True)
        gate_values = jnp.dot(everyone, w_gate[e], preferred_element_type=jnp.float32)
        up_values = jnp.dot(everyone, w_up[e], preferred_element_type=jnp.float32)
        activated = (jax.nn.silu(gate_values) * up_values).astype(jnp.bfloat16)
        partial = partial + scale * jnp.dot(
            activated, w_down[e], preferred_element_type=jnp.float32
        )
    return finish(
        devices,
        capacity,
        partial.astype(jnp.bfloat16),
        hidden,
        picks,
        talk_gain,
        codec_state,
        w_talk,
    )


def solution(mesh):
    both = ("parts", "expert")
    in_specs = (
        P(both, None),
        P(both, None, None),
        P(both, None),
        P(both, None),
        P(both),
        P(both, None),
        P(),
        P(),
        P("expert", None, None),
        P("expert", None, None),
        P("expert", None, None),
        P(both, None),
        P(both, None),
        P(both),
        P(both),
        P(both, None),
        P(),
        P(),
    )
    out_specs = (P(both, None), P(both, None))
    return jax.shard_map(body, mesh=mesh, in_specs=in_specs, out_specs=out_specs, check_vma=False)
```

```python
import functools
import math

import jax
import jax.numpy as jnp
from jax import lax
from jax.experimental import pallas as pl
from jax.experimental.pallas import tpu as pltpu
from jax.sharding import PartitionSpec as P

HD = 128
STACK = 4
NEG = -1e30
LOG2E = 1.4426950408889634


def attend_kernel(
    kv_heads,
    page,
    q_ref,
    kv_ref,
    fresh_ref,
    table_ref,
    len_ref,
    resid_ref,
    wout_ref,
    gain_ref,
    hidden_ref,
    normed_ref,
    bias_ref,
    att_ref,
):
    rows, qwidth = q_ref.shape
    tokens = kv_ref.shape[0]
    pages = tokens // page
    max_pages = table_ref.shape[1]
    heads = qwidth // HD
    per_kv = heads // kv_heads
    factor = LOG2E / math.sqrt(HD)

    lengths = len_ref[...]
    page_ids = lax.broadcasted_iota(jnp.int32, (rows, pages), 1)
    whole = jnp.zeros((rows, pages), jnp.float32)
    last = jnp.zeros((rows, pages), jnp.float32)
    for j in range(max_pages):
        named = page_ids == table_ref[:, j : j + 1]
        whole += jnp.where(named & (lengths >= page * (j + 1)), 1.0, 0.0)
        last += jnp.where(
            named & (lengths > page * j) & (lengths < page * (j + 1)), 1.0, 0.0
        )
    spread = jnp.where(
        lax.broadcasted_iota(jnp.int32, (pages, tokens), 1) // page
        == lax.broadcasted_iota(jnp.int32, (pages, tokens), 0),
        1.0,
        0.0,
    ).astype(jnp.bfloat16)
    whole_tok = jnp.dot(whole.astype(jnp.bfloat16), spread, preferred_element_type=jnp.float32)
    last_tok = jnp.dot(last.astype(jnp.bfloat16), spread, preferred_element_type=jnp.float32)
    place = lax.rem(lax.broadcasted_iota(jnp.int32, (rows, tokens), 1), page)
    times = whole_tok + jnp.where(place < lax.rem(lengths, page), last_tok, 0.0)
    bias_ref[...] = jnp.where(times > 0.5, jnp.log2(jnp.maximum(times, 1.0)), NEG)

    def step(i, carry):
        kvh = (i * STACK) // per_kv
        lanes = pl.ds(pl.multiple_of(i * STACK * HD, STACK * HD), STACK * HD)
        keys = pl.ds(pl.multiple_of(kvh * HD, HD), HD)
        vals = pl.ds(pl.multiple_of((kv_heads + kvh) * HD, HD), HD)
        qs = q_ref[:, lanes]
        stacked = jnp.concatenate([qs[:, h * HD : (h + 1) * HD] for h in range(STACK)], axis=0)
        scores = lax.dot_general(
            stacked, kv_ref[:, keys], (((1,), (1,)), ((), ())), preferred_element_type=jnp.float32
        )
        fresh_key = fresh_ref[:, keys].astype(jnp.float32)
        fresh_val = fresh_ref[:, vals].astype(jnp.float32)
        wide = stacked.astype(jnp.float32).reshape(STACK, rows, HD)
        own = jnp.sum(wide * fresh_key[None], axis=-1, keepdims=True) * factor
        logits = scores.reshape(STACK, rows, tokens) * factor + bias_ref[...][None]
        highest = jnp.maximum(jnp.max(logits, axis=-1, keepdims=True), own)
        weights = jnp.exp2(logits - highest)
        own_weight = jnp.exp2(own - highest)
        denom = jnp.sum(weights, axis=-1, keepdims=True) + own_weight
        mixed = jnp.dot(
            weights.astype(jnp.bfloat16).reshape(STACK * rows, tokens),
            kv_ref[:, vals],
            preferred_element_type=jnp.float32,
        ).reshape(STACK, rows, HD)
        mixed = ((mixed + own_weight * fresh_val[None]) / denom).astype(jnp.bfloat16)
        att_ref[:, lanes] = jnp.concatenate([mixed[h] for h in range(STACK)], axis=1)
        return carry

    lax.fori_loop(0, heads // STACK, step, 0)
    hidden = (
        resid_ref[...].astype(jnp.float32)
        + jnp.dot(att_ref[...], wout_ref[...], preferred_element_type=jnp.float32)
    ).astype(jnp.bfloat16)
    hidden_ref[...] = hidden
    normed_ref[...] = rms_scaled(hidden, gain_ref[...]).astype(jnp.bfloat16)


def rms_scaled(values, gain_row):
    widened = values.astype(jnp.float32)
    return (
        widened * lax.rsqrt(jnp.mean(widened * widened, axis=-1, keepdims=True) + 1e-06) * gain_row
    )


def attend(queries, kv_cache, new_kv, page_table, ctx_len, resid, w_out, moe_gain):
    rows, width = resid.shape
    pages, page, kv_width = kv_cache.shape
    tokens = pages * page
    shape = jax.ShapeDtypeStruct((rows, width), jnp.bfloat16)
    return pl.pallas_call(
        functools.partial(attend_kernel, kv_width // (2 * HD), page),
        out_shape=(shape, shape),
        in_specs=[pl.BlockSpec(memory_space=pltpu.VMEM)] * 8,
        out_specs=(pl.BlockSpec(memory_space=pltpu.VMEM),) * 2,
        scratch_shapes=[
            pltpu.VMEM((rows, tokens), jnp.float32),
            pltpu.VMEM((rows, queries.shape[1]), jnp.bfloat16),
        ],
        compiler_params=pltpu.CompilerParams(vmem_limit_bytes=48 * 1024 * 1024),
        cost_estimate=pl.CostEstimate(
            flops=4 * rows * queries.shape[1] * tokens,
            bytes_accessed=2 * (tokens * kv_width + w_out.size + 4 * resid.size),
            transcendentals=0,
        ),
    )(
        queries,
        kv_cache.reshape(tokens, kv_width),
        new_kv,
        page_table,
        ctx_len[:, None],
        resid,
        w_out,
        moe_gain[None, :],
    )


def flipped(me, bits, total):
    out, stride = 0, 1
    while stride < total:
        bit = (me // stride) % 2
        out = out + stride * ((1 - bit) if bits & stride else bit)
        stride *= 2
    return out


def gather_kernel(n, own_ref, out_ref, send_sem, recv_sem):
    wide = own_ref.shape[1]
    first = -(-wide // 256) * 128
    spans = ((0, first), (first, wide - first))
    me = lax.axis_index("expert")
    strides = [1 << b for b in range(n.bit_length() - 1)]
    orders = (strides[::-1], strides[1:2] + strides[:1:-1] + strides[:1])
    barrier = pltpu.get_barrier_semaphore()
    for s in strides:
        pl.semaphore_signal(
            barrier,
            inc=1,
            device_id={"expert": flipped(me, s, n)},
            device_id_type=pl.DeviceIdType.MESH,
        )
    out_ref[pl.ds(me, 1)] = own_ref[...][None]
    pl.semaphore_wait(barrier, len(strides))

    def message(half, m, s):
        block = out_ref.at[flipped(me, m - s, n), :, pl.ds(*spans[half])]
        return pltpu.make_async_remote_copy(
            src_ref=block,
            dst_ref=block,
            send_sem=send_sem.at[half, m],
            recv_sem=recv_sem.at[half, m],
            device_id={"expert": flipped(me, s, n)},
            device_id_type=pl.DeviceIdType.MESH,
        )

    sent, held, waited = {}, ([0], [0]), set()
    for k in range(len(strides)):
        added = ([], [])
        for place in range(1 << k):
            for half in range(2):
                s, r = orders[half][k], held[half][place]
                if r and (half, r) not in waited:
                    sent[half, r].wait_recv()
                    waited.add((half, r))
                sent[half, r + s] = message(half, r + s, s)
                sent[half, r + s].start()
                added[half].append(r + s)
        for half in range(2):
            held[half].extend(added[half])
    for key, copy in sent.items():
        if key not in waited:
            copy.wait_recv()
        copy.wait_send()


def gather_rows(n, own):
    return pl.pallas_call(
        functools.partial(gather_kernel, n),
        out_shape=jax.ShapeDtypeStruct((n,) + own.shape, own.dtype),
        in_specs=[pl.BlockSpec(memory_space=pltpu.VMEM)],
        out_specs=pl.BlockSpec(memory_space=pltpu.VMEM),
        scratch_shapes=[pltpu.SemaphoreType.DMA((2, n)), pltpu.SemaphoreType.DMA((2, n))],
        compiler_params=pltpu.CompilerParams(
            collective_id=1, has_side_effects=True, vmem_limit_bytes=40 * 1024 * 1024
        ),
    )(own).reshape(n * own.shape[0], own.shape[1])


def finish_kernel(
    n,
    capacity,
    part_ref,
    hidden_ref,
    picks_ref,
    gain_ref,
    codec_ref,
    wtalk_ref,
    thinker_ref,
    talker_ref,
    stage,
    landed,
    voice_out,
    voice_in,
    send_sem,
    recv_sem,
    voice_send,
    voice_recv,
):
    rows, width = hidden_ref.shape
    cols = width // 2
    room = voice_out.shape[1]
    me = lax.axis_index("expert")
    barrier = pltpu.get_barrier_semaphore()

    def greet(i, carry):
        peer = (me + i) % n
        pl.semaphore_signal(
            barrier, inc=1, device_id={"expert": peer}, device_id_type=pl.DeviceIdType.MESH
        )
        return carry

    lax.fori_loop(1, n, greet, 0)
    pl.semaphore_wait(barrier, n - 1)

    strides = [1 << b for b in range(n.bit_length() - 1)]
    orders = (strides, strides[:1] + strides[2:] + strides[1:2])

    def step_of(half, r):
        return next(k for k, s in enumerate(orders[half]) if r & s)

    def message(half, r, source):
        partner = flipped(me, orders[half][step_of(half, r)], n)
        return pltpu.make_async_remote_copy(
            src_ref=source,
            dst_ref=landed.at[half, r],
            send_sem=send_sem.at[half, r],
            recv_sem=recv_sem.at[half, r],
            device_id={"expert": partner},
            device_id_type=pl.DeviceIdType.MESH,
        )

    def summed(half, r, k):
        lanes = slice(half * cols, (half + 1) * cols)
        total = part_ref[flipped(me, r, n), :, lanes].astype(jnp.float32)
        for j in range(k):
            m = r + orders[half][j]
            sent[half, m].wait_recv()
            total = total + landed[half, m].astype(jnp.float32)
        return total

    sent = {}
    for k in range(len(strides)):
        for half in range(2):
            todo = [r for r in range(1, n) if step_of(half, r) == k]
            nearer = orders[half][k + 1 :]
            todo.sort(key=lambda r: [-((r & s) > 0) for s in nearer])
            for r in todo:
                if k == 0:
                    source = part_ref.at[flipped(me, r, n), :, pl.ds(half * cols, cols)]
                else:
                    stage[half, r] = summed(half, r, k).astype(jnp.bfloat16)
                    source = stage.at[half, r]
                sent[half, r] = message(half, r, source)
                sent[half, r].start()
    mixture = jnp.concatenate([summed(half, 0, len(strides)) for half in range(2)], axis=1)
    thinker = (hidden_ref[...].astype(jnp.float32) + mixture).astype(jnp.bfloat16)
    thinker_ref[...] = thinker
    voice = rms_scaled(thinker, gain_ref[...]).astype(jnp.bfloat16)
    packed = jnp.dot(picks_ref[0], voice[:, :cols], preferred_element_type=jnp.float32) + jnp.dot(
        picks_ref[1], voice[:, cols:], preferred_element_type=jnp.float32
    )
    voice_out[...] = packed.astype(jnp.bfloat16).reshape(n, room, cols)
    voice_in[pl.ds(me, 1)] = voice_out[pl.ds(me, 1)]

    def voice_copy(i):
        peer = (me + i) % n
        return pltpu.make_async_remote_copy(
            src_ref=voice_out.at[peer],
            dst_ref=voice_in.at[me],
            send_sem=voice_send.at[i],
            recv_sem=voice_recv.at[i],
            device_id={"expert": peer},
            device_id_type=pl.DeviceIdType.MESH,
        )

    def begin(i, carry):
        voice_copy(i).start()
        return carry

    def end(i, carry):
        copy = voice_copy(i)
        copy.wait_send()
        copy.wait_recv()
        return carry

    lax.fori_loop(1, n, begin, 0)
    for copy in sent.values():
        copy.wait_send()
    lax.fori_loop(1, n, end, 0)
    arrived = voice_in[...].reshape(n * room, cols)
    slot = lax.broadcasted_iota(jnp.int32, (n * capacity, n * room), 0)
    place = lax.broadcasted_iota(jnp.int32, (n * capacity, n * room), 1)
    near = (slot // capacity) * room + lax.rem(slot, capacity)
    total = codec_ref[...].astype(jnp.float32)
    for half in range(2):
        chosen = jnp.where(place == near + half * (room // 2), 1.0, 0.0).astype(jnp.bfloat16)
        part = jnp.dot(chosen, arrived, preferred_element_type=jnp.float32).astype(jnp.bfloat16)
        total = total + jnp.dot(
            part, wtalk_ref[half * cols : (half + 1) * cols, :], preferred_element_type=jnp.float32
        )
    talker_ref[...] = total.astype(jnp.bfloat16)


def finish(n, capacity, partial, hidden, picks, talk_gain, codec_state, w_talk):
    rows, width = hidden.shape
    room = picks.shape[1] // n
    cols = width // 2
    return pl.pallas_call(
        functools.partial(finish_kernel, n, capacity),
        out_shape=(
            jax.ShapeDtypeStruct((rows, width), jnp.bfloat16),
            jax.ShapeDtypeStruct(codec_state.shape, jnp.bfloat16),
        ),
        in_specs=[pl.BlockSpec(memory_space=pltpu.VMEM)] * 6,
        out_specs=(pl.BlockSpec(memory_space=pltpu.VMEM),) * 2,
        scratch_shapes=[
            pltpu.VMEM((2, n, rows, cols), jnp.bfloat16),
            pltpu.VMEM((2, n, rows, cols), jnp.bfloat16),
            pltpu.VMEM((n, room, cols), jnp.bfloat16),
            pltpu.VMEM((n, room, cols), jnp.bfloat16),
            pltpu.SemaphoreType.DMA((2, n)),
            pltpu.SemaphoreType.DMA((2, n)),
            pltpu.SemaphoreType.DMA((n,)),
            pltpu.SemaphoreType.DMA((n,)),
        ],
        compiler_params=pltpu.CompilerParams(
            collective_id=0, has_side_effects=True, vmem_limit_bytes=56 * 1024 * 1024
        ),
    )(partial.reshape(n, rows, width), hidden, picks, talk_gain[None, :], codec_state, w_talk)


def talker_picks(owners, voiced, devices, capacity):
    row_total = owners.shape[0]
    span = -(-capacity // 8) * 8
    one_hot = (owners[:, None] == jnp.arange(devices, dtype=jnp.int32)[None, :]) & (
        voiced[:, None] == 1
    )
    order = jnp.arange(row_total, dtype=jnp.int32)
    before = (order[None, :] < order[:, None]).astype(jnp.bfloat16)
    counts = jnp.dot(before, one_hot.astype(jnp.bfloat16), preferred_element_type=jnp.float32)
    earlier = jnp.sum(jnp.where(one_hot, counts, 0.0), axis=1).astype(jnp.int32)
    room = 2 * span
    target = jnp.where(voiced == 1, owners * room + earlier, -room)
    slots = jnp.arange(devices * room, dtype=jnp.int32)
    return jnp.stack(
        [
            (slots[:, None] == target[None, :] + half * span).astype(jnp.bfloat16)
            for half in range(2)
        ]
    )


def body(
    queries,
    kv_cache,
    new_kv,
    page_table,
    ctx_len,
    resid,
    w_out,
    moe_gain,
    w_gate,
    w_up,
    w_down,
    routes,
    route_weight,
    talker_owner,
    speaking,
    codec_state,
    talk_gain,
    w_talk,
):
    devices = lax.axis_size("expert")
    capacity = codec_state.shape[0] // devices
    local = w_gate.shape[0]
    experts = local * devices
    width = resid.shape[1]
    dense = jnp.sum(
        jnp.where(
            routes[:, :, None] == jnp.arange(experts, dtype=jnp.int32)[None, None, :],
            route_weight[:, :, None],
            0.0,
        ),
        axis=1,
    )
    coarse = lax.reduce_precision(dense, 8, 7)
    wide = -(-2 * experts // 128) * 128
    riders = jnp.concatenate([coarse, dense - coarse], axis=1).astype(jnp.bfloat16)
    riders = jnp.pad(riders, ((0, 0), (0, wide - 2 * experts)))
    picks = talker_picks(talker_owner, speaking, devices, capacity)
    hidden, normed = attend(
        queries, kv_cache, new_kv, page_table, ctx_len, resid, w_out, moe_gain
    )
    gathered = gather_rows(devices, jnp.concatenate([normed, riders], axis=1))
    everyone = gathered[:, :width]
    shares = gathered[:, width : width + 2 * experts].astype(jnp.float32)
    me = lax.axis_index("expert")
    partial = 0.0
    for e in range(local):
        mine = jnp.arange(2 * experts, dtype=jnp.int32) % experts == me * local + e
        scale = jnp.sum(jnp.where(mine[None, :], shares, 0.0), axis=1, keepdims=True)
        gate_values = jnp.dot(everyone, w_gate[e], preferred_element_type=jnp.float32)
        up_values = jnp.dot(everyone, w_up[e], preferred_element_type=jnp.float32)
        activated = (jax.nn.silu(gate_values) * up_values).astype(jnp.bfloat16)
        partial = partial + scale * jnp.dot(
            activated, w_down[e], preferred_element_type=jnp.float32
        )
    return finish(
        devices,
        capacity,
        partial.astype(jnp.bfloat16),
        hidden,
        picks,
        talk_gain,
        codec_state,
        w_talk,
    )


def solution(mesh):
    both = ("parts", "expert")
    in_specs = (
        P(both, None),
        P(both, None, None),
        P(both, None),
        P(both, None),
        P(both),
        P(both, None),
        P(),
        P(),
        P("expert", None, None),
        P("expert", None, None),
        P("expert", None, None),
        P(both, None),
        P(both, None),
        P(both),
        P(both),
        P(both, None),
        P(),
        P(),
    )
    out_specs = (P(both, None), P(both, None))
    return jax.shard_map(body, mesh=mesh, in_specs=in_specs, out_specs=out_specs, check_vma=False)
```

```python
import functools
import math

import jax
import jax.numpy as jnp
from jax import lax
from jax.experimental import pallas as pl
from jax.experimental.pallas import tpu as pltpu
from jax.sharding import PartitionSpec as P

HD = 128
STACK = 4
NEG = -1e30
LOG2E = 1.4426950408889634


def attend_kernel(
    kv_heads,
    page,
    q_ref,
    kv_ref,
    fresh_ref,
    table_ref,
    len_ref,
    resid_ref,
    wout_ref,
    gain_ref,
    hidden_ref,
    normed_ref,
    bias_ref,
    att_ref,
):
    rows, qwidth = q_ref.shape
    tokens = kv_ref.shape[0]
    pages = tokens // page
    max_pages = table_ref.shape[1]
    heads = qwidth // HD
    per_kv = heads // kv_heads
    factor = LOG2E / math.sqrt(HD)

    lengths = len_ref[...]
    page_ids = lax.broadcasted_iota(jnp.int32, (rows, pages), 1)
    whole = jnp.zeros((rows, pages), jnp.float32)
    last = jnp.zeros((rows, pages), jnp.float32)
    for j in range(max_pages):
        named = page_ids == table_ref[:, j : j + 1]
        whole += jnp.where(named & (lengths >= page * (j + 1)), 1.0, 0.0)
        last += jnp.where(
            named & (lengths > page * j) & (lengths < page * (j + 1)), 1.0, 0.0
        )
    spread = jnp.where(
        lax.broadcasted_iota(jnp.int32, (pages, tokens), 1) // page
        == lax.broadcasted_iota(jnp.int32, (pages, tokens), 0),
        1.0,
        0.0,
    ).astype(jnp.bfloat16)
    whole_tok = jnp.dot(whole.astype(jnp.bfloat16), spread, preferred_element_type=jnp.float32)
    last_tok = jnp.dot(last.astype(jnp.bfloat16), spread, preferred_element_type=jnp.float32)
    place = lax.rem(lax.broadcasted_iota(jnp.int32, (rows, tokens), 1), page)
    times = whole_tok + jnp.where(place < lax.rem(lengths, page), last_tok, 0.0)
    bias_ref[...] = jnp.where(times > 0.5, jnp.log2(jnp.maximum(times, 1.0)), NEG)

    def step(i, carry):
        kvh = (i * STACK) // per_kv
        lanes = pl.ds(pl.multiple_of(i * STACK * HD, STACK * HD), STACK * HD)
        keys = pl.ds(pl.multiple_of(kvh * HD, HD), HD)
        vals = pl.ds(pl.multiple_of((kv_heads + kvh) * HD, HD), HD)
        qs = q_ref[:, lanes]
        stacked = jnp.concatenate([qs[:, h * HD : (h + 1) * HD] for h in range(STACK)], axis=0)
        scores = lax.dot_general(
            stacked, kv_ref[:, keys], (((1,), (1,)), ((), ())), preferred_element_type=jnp.float32
        )
        fresh_key = fresh_ref[:, keys].astype(jnp.float32)
        fresh_val = fresh_ref[:, vals].astype(jnp.float32)
        wide = stacked.astype(jnp.float32).reshape(STACK, rows, HD)
        own = jnp.sum(wide * fresh_key[None], axis=-1, keepdims=True) * factor
        logits = scores.reshape(STACK, rows, tokens) * factor + bias_ref[...][None]
        highest = jnp.maximum(jnp.max(logits, axis=-1, keepdims=True), own)
        weights = jnp.exp2(logits - highest)
        own_weight = jnp.exp2(own - highest)
        denom = jnp.sum(weights, axis=-1, keepdims=True) + own_weight
        mixed = jnp.dot(
            weights.astype(jnp.bfloat16).reshape(STACK * rows, tokens),
            kv_ref[:, vals],
            preferred_element_type=jnp.float32,
        ).reshape(STACK, rows, HD)
        mixed = ((mixed + own_weight * fresh_val[None]) / denom).astype(jnp.bfloat16)
        att_ref[:, lanes] = jnp.concatenate([mixed[h] for h in range(STACK)], axis=1)
        return carry

    lax.fori_loop(0, heads // STACK, step, 0)
    hidden = (
        resid_ref[...].astype(jnp.float32)
        + jnp.dot(att_ref[...], wout_ref[...], preferred_element_type=jnp.float32)
    ).astype(jnp.bfloat16)
    hidden_ref[...] = hidden
    normed_ref[...] = rms_scaled(hidden, gain_ref[...]).astype(jnp.bfloat16)


def rms_scaled(values, gain_row):
    widened = values.astype(jnp.float32)
    return (
        widened * lax.rsqrt(jnp.mean(widened * widened, axis=-1, keepdims=True) + 1e-06) * gain_row
    )


def attend(queries, kv_cache, new_kv, page_table, ctx_len, resid, w_out, moe_gain):
    rows, width = resid.shape
    pages, page, kv_width = kv_cache.shape
    tokens = pages * page
    shape = jax.ShapeDtypeStruct((rows, width), jnp.bfloat16)
    return pl.pallas_call(
        functools.partial(attend_kernel, kv_width // (2 * HD), page),
        out_shape=(shape, shape),
        in_specs=[pl.BlockSpec(memory_space=pltpu.VMEM)] * 8,
        out_specs=(pl.BlockSpec(memory_space=pltpu.VMEM),) * 2,
        scratch_shapes=[
            pltpu.VMEM((rows, tokens), jnp.float32),
            pltpu.VMEM((rows, queries.shape[1]), jnp.bfloat16),
        ],
        compiler_params=pltpu.CompilerParams(vmem_limit_bytes=48 * 1024 * 1024),
        cost_estimate=pl.CostEstimate(
            flops=4 * rows * queries.shape[1] * tokens,
            bytes_accessed=2 * (tokens * kv_width + w_out.size + 4 * resid.size),
            transcendentals=0,
        ),
    )(
        queries,
        kv_cache.reshape(tokens, kv_width),
        new_kv,
        page_table,
        ctx_len[:, None],
        resid,
        w_out,
        moe_gain[None, :],
    )


def flipped(me, bits, total):
    out, stride = 0, 1
    while stride < total:
        bit = (me // stride) % 2
        out = out + stride * ((1 - bit) if bits & stride else bit)
        stride *= 2
    return out


def gather_kernel(n, own_ref, out_ref, send_sem, recv_sem):
    wide = own_ref.shape[1]
    first = -(-wide // 256) * 128
    spans = ((0, first), (first, wide - first))
    me = lax.axis_index("expert")
    strides = [1 << b for b in range(n.bit_length() - 1)]
    orders = (strides[::-1], strides[1:2] + strides[:1:-1] + strides[:1])
    barrier = pltpu.get_barrier_semaphore()
    for s in strides:
        pl.semaphore_signal(
            barrier,
            inc=1,
            device_id={"expert": flipped(me, s, n)},
            device_id_type=pl.DeviceIdType.MESH,
        )
    out_ref[pl.ds(me, 1)] = own_ref[...][None]
    pl.semaphore_wait(barrier, len(strides))

    def message(half, m, s):
        block = out_ref.at[flipped(me, m - s, n), :, pl.ds(*spans[half])]
        return pltpu.make_async_remote_copy(
            src_ref=block,
            dst_ref=block,
            send_sem=send_sem.at[half, m],
            recv_sem=recv_sem.at[half, m],
            device_id={"expert": flipped(me, s, n)},
            device_id_type=pl.DeviceIdType.MESH,
        )

    sent, held, waited = {}, ([0], [0]), set()
    for k in range(len(strides)):
        added = ([], [])
        for place in range(1 << k):
            for half in range(2):
                s, r = orders[half][k], held[half][place]
                if r and (half, r) not in waited:
                    sent[half, r].wait_recv()
                    waited.add((half, r))
                sent[half, r + s] = message(half, r + s, s)
                sent[half, r + s].start()
                added[half].append(r + s)
        for half in range(2):
            held[half].extend(added[half])
    for key, copy in sent.items():
        if key not in waited:
            copy.wait_recv()
        copy.wait_send()


def gather_rows(n, own):
    return pl.pallas_call(
        functools.partial(gather_kernel, n),
        out_shape=jax.ShapeDtypeStruct((n,) + own.shape, own.dtype),
        in_specs=[pl.BlockSpec(memory_space=pltpu.VMEM)],
        out_specs=pl.BlockSpec(memory_space=pltpu.VMEM),
        scratch_shapes=[pltpu.SemaphoreType.DMA((2, n)), pltpu.SemaphoreType.DMA((2, n))],
        compiler_params=pltpu.CompilerParams(
            collective_id=1, has_side_effects=True, vmem_limit_bytes=40 * 1024 * 1024
        ),
    )(own).reshape(n * own.shape[0], own.shape[1])


def finish_kernel(
    n,
    capacity,
    part_ref,
    hidden_ref,
    picks_ref,
    gain_ref,
    codec_ref,
    wtalk_ref,
    thinker_ref,
    talker_ref,
    stage,
    landed,
    voice_out,
    voice_in,
    send_sem,
    recv_sem,
    voice_send,
    voice_recv,
):
    rows, width = hidden_ref.shape
    cols = width // 2
    room = voice_out.shape[1]
    me = lax.axis_index("expert")
    barrier = pltpu.get_barrier_semaphore()

    def greet(i, carry):
        peer = (me + i) % n
        pl.semaphore_signal(
            barrier, inc=1, device_id={"expert": peer}, device_id_type=pl.DeviceIdType.MESH
        )
        return carry

    lax.fori_loop(1, n, greet, 0)
    pl.semaphore_wait(barrier, n - 1)

    strides = [1 << b for b in range(n.bit_length() - 1)]
    orders = (strides, strides[:1] + strides[2:] + strides[1:2])

    def step_of(half, r):
        return next(k for k, s in enumerate(orders[half]) if r & s)

    def message(half, r, source):
        partner = flipped(me, orders[half][step_of(half, r)], n)
        return pltpu.make_async_remote_copy(
            src_ref=source,
            dst_ref=landed.at[half, r],
            send_sem=send_sem.at[half, r],
            recv_sem=recv_sem.at[half, r],
            device_id={"expert": partner},
            device_id_type=pl.DeviceIdType.MESH,
        )

    def summed(half, r, k):
        lanes = slice(half * cols, (half + 1) * cols)
        total = part_ref[flipped(me, r, n), :, lanes].astype(jnp.float32)
        for j in range(k):
            m = r + orders[half][j]
            sent[half, m].wait_recv()
            total = total + landed[half, m].astype(jnp.float32)
        return total

    sent = {}
    for k in range(len(strides)):
        todo = []
        for half in range(2):
            now = [r for r in range(1, n) if step_of(half, r) == k]
            nearer = orders[half][k + 1 :]
            now.sort(key=lambda r: [-((r & s) > 0) for s in nearer])
            todo.append([(half, r) for r in now])
        for half, r in [one for pair in zip(*todo) for one in pair]:
            if k == 0:
                source = part_ref.at[flipped(me, r, n), :, pl.ds(half * cols, cols)]
            else:
                stage[half, r] = summed(half, r, k).astype(jnp.bfloat16)
                source = stage.at[half, r]
            sent[half, r] = message(half, r, source)
            sent[half, r].start()
    mixture = jnp.concatenate([summed(half, 0, len(strides)) for half in range(2)], axis=1)
    thinker = (hidden_ref[...].astype(jnp.float32) + mixture).astype(jnp.bfloat16)
    thinker_ref[...] = thinker
    voice = rms_scaled(thinker, gain_ref[...]).astype(jnp.bfloat16)
    packed = jnp.dot(picks_ref[0], voice[:, :cols], preferred_element_type=jnp.float32) + jnp.dot(
        picks_ref[1], voice[:, cols:], preferred_element_type=jnp.float32
    )
    voice_out[...] = packed.astype(jnp.bfloat16).reshape(n, room, cols)
    voice_in[pl.ds(me, 1)] = voice_out[pl.ds(me, 1)]

    def voice_copy(i):
        peer = (me + i) % n
        return pltpu.make_async_remote_copy(
            src_ref=voice_out.at[peer],
            dst_ref=voice_in.at[me],
            send_sem=voice_send.at[i],
            recv_sem=voice_recv.at[i],
            device_id={"expert": peer},
            device_id_type=pl.DeviceIdType.MESH,
        )

    def begin(i, carry):
        voice_copy(i).start()
        return carry

    def end(i, carry):
        copy = voice_copy(i)
        copy.wait_send()
        copy.wait_recv()
        return carry

    lax.fori_loop(1, n, begin, 0)
    for copy in sent.values():
        copy.wait_send()
    lax.fori_loop(1, n, end, 0)
    arrived = voice_in[...].reshape(n * room, cols)
    slot = lax.broadcasted_iota(jnp.int32, (n * capacity, n * room), 0)
    place = lax.broadcasted_iota(jnp.int32, (n * capacity, n * room), 1)
    near = (slot // capacity) * room + lax.rem(slot, capacity)
    total = codec_ref[...].astype(jnp.float32)
    for half in range(2):
        chosen = jnp.where(place == near + half * (room // 2), 1.0, 0.0).astype(jnp.bfloat16)
        part = jnp.dot(chosen, arrived, preferred_element_type=jnp.float32).astype(jnp.bfloat16)
        total = total + jnp.dot(
            part, wtalk_ref[half * cols : (half + 1) * cols, :], preferred_element_type=jnp.float32
        )
    talker_ref[...] = total.astype(jnp.bfloat16)


def finish(n, capacity, partial, hidden, picks, talk_gain, codec_state, w_talk):
    rows, width = hidden.shape
    room = picks.shape[1] // n
    cols = width // 2
    return pl.pallas_call(
        functools.partial(finish_kernel, n, capacity),
        out_shape=(
            jax.ShapeDtypeStruct((rows, width), jnp.bfloat16),
            jax.ShapeDtypeStruct(codec_state.shape, jnp.bfloat16),
        ),
        in_specs=[pl.BlockSpec(memory_space=pltpu.VMEM)] * 6,
        out_specs=(pl.BlockSpec(memory_space=pltpu.VMEM),) * 2,
        scratch_shapes=[
            pltpu.VMEM((2, n, rows, cols), jnp.bfloat16),
            pltpu.VMEM((2, n, rows, cols), jnp.bfloat16),
            pltpu.VMEM((n, room, cols), jnp.bfloat16),
            pltpu.VMEM((n, room, cols), jnp.bfloat16),
            pltpu.SemaphoreType.DMA((2, n)),
            pltpu.SemaphoreType.DMA((2, n)),
            pltpu.SemaphoreType.DMA((n,)),
            pltpu.SemaphoreType.DMA((n,)),
        ],
        compiler_params=pltpu.CompilerParams(
            collective_id=0, has_side_effects=True, vmem_limit_bytes=56 * 1024 * 1024
        ),
    )(partial.reshape(n, rows, width), hidden, picks, talk_gain[None, :], codec_state, w_talk)


def talker_picks(owners, voiced, devices, capacity):
    row_total = owners.shape[0]
    span = -(-capacity // 8) * 8
    one_hot = (owners[:, None] == jnp.arange(devices, dtype=jnp.int32)[None, :]) & (
        voiced[:, None] == 1
    )
    order = jnp.arange(row_total, dtype=jnp.int32)
    before = (order[None, :] < order[:, None]).astype(jnp.bfloat16)
    counts = jnp.dot(before, one_hot.astype(jnp.bfloat16), preferred_element_type=jnp.float32)
    earlier = jnp.sum(jnp.where(one_hot, counts, 0.0), axis=1).astype(jnp.int32)
    room = 2 * span
    target = jnp.where(voiced == 1, owners * room + earlier, -room)
    slots = jnp.arange(devices * room, dtype=jnp.int32)
    return jnp.stack(
        [
            (slots[:, None] == target[None, :] + half * span).astype(jnp.bfloat16)
            for half in range(2)
        ]
    )


def body(
    queries,
    kv_cache,
    new_kv,
    page_table,
    ctx_len,
    resid,
    w_out,
    moe_gain,
    w_gate,
    w_up,
    w_down,
    routes,
    route_weight,
    talker_owner,
    speaking,
    codec_state,
    talk_gain,
    w_talk,
):
    devices = lax.axis_size("expert")
    capacity = codec_state.shape[0] // devices
    local = w_gate.shape[0]
    experts = local * devices
    width = resid.shape[1]
    dense = jnp.sum(
        jnp.where(
            routes[:, :, None] == jnp.arange(experts, dtype=jnp.int32)[None, None, :],
            route_weight[:, :, None],
            0.0,
        ),
        axis=1,
    )
    coarse = lax.reduce_precision(dense, 8, 7)
    wide = -(-2 * experts // 128) * 128
    riders = jnp.concatenate([coarse, dense - coarse], axis=1).astype(jnp.bfloat16)
    riders = jnp.pad(riders, ((0, 0), (0, wide - 2 * experts)))
    picks = talker_picks(talker_owner, speaking, devices, capacity)
    hidden, normed = attend(
        queries, kv_cache, new_kv, page_table, ctx_len, resid, w_out, moe_gain
    )
    gathered = gather_rows(devices, jnp.concatenate([normed, riders], axis=1))
    everyone = gathered[:, :width]
    shares = gathered[:, width : width + 2 * experts].astype(jnp.float32)
    me = lax.axis_index("expert")
    partial = 0.0
    for e in range(local):
        mine = jnp.arange(2 * experts, dtype=jnp.int32) % experts == me * local + e
        scale = jnp.sum(jnp.where(mine[None, :], shares, 0.0), axis=1, keepdims=True)
        gate_values = jnp.dot(everyone, w_gate[e], preferred_element_type=jnp.float32)
        up_values = jnp.dot(everyone, w_up[e], preferred_element_type=jnp.float32)
        activated = (jax.nn.silu(gate_values) * up_values).astype(jnp.bfloat16)
        partial = partial + scale * jnp.dot(
            activated, w_down[e], preferred_element_type=jnp.float32
        )
    return finish(
        devices,
        capacity,
        partial.astype(jnp.bfloat16),
        hidden,
        picks,
        talk_gain,
        codec_state,
        w_talk,
    )


def solution(mesh):
    both = ("parts", "expert")
    in_specs = (
        P(both, None),
        P(both, None, None),
        P(both, None),
        P(both, None),
        P(both),
        P(both, None),
        P(),
        P(),
        P("expert", None, None),
        P("expert", None, None),
        P("expert", None, None),
        P(both, None),
        P(both, None),
        P(both),
        P(both),
        P(both, None),
        P(),
        P(),
    )
    out_specs = (P(both, None), P(both, None))
    return jax.shard_map(body, mesh=mesh, in_specs=in_specs, out_specs=out_specs, check_vma=False)
```
